256 devices in a mesh: row: 2 (over core), col: 16 (over y, x), depth: 8 (over z).
Axes of the slice: x: 4, y: 4, z: 8, core: 2. Of those that a mesh axis runs over, the one named last changes fastest.
Arguments:
- tokens_in: bfloat16 [8192, 2560], P(('row', 'depth'), 'col'), may hold values from -6 to 6
- w_in: bfloat16 [2560, 10240], P('row', 'col'), may hold values from -0.15625 to 0.15625
- w_out: bfloat16 [2560, 10240], P('row', 'col'), may hold values from -0.078125 to 0.078125
- grad_out: bfloat16 [8192, 2560], P(('row', 'depth'), 'col'), may hold values from -3 to 3
Outputs:
- block_out: bfloat16 [8192, 2560], P(('row', 'depth'), 'col')
- grad_tokens: bfloat16 [8192, 2560], P(('row', 'depth'), 'col')
- grad_w_in: bfloat16 [2560, 10240], P('row', 'col')
- grad_w_out: bfloat16 [2560, 10240], P('row', 'col')
The draws below stay inside these ranges and needn't reach their ends.
All inputs are finite; a program needn't handle non-finite values.
Results may differ from the reference program's by a relative error of at most 0.023.
Values may be sent and summed in bfloat16 or wider, within the bound.
A program may use at most 128 MiB of HBM per device.

```python
import jax
import jax.numpy as jnp
from jax import lax

D = 2560
FF = 10240
TOKENS = 8192
N_ROW = 2
N_COL = 16
N_DEPTH = 8


def raised(result, key, source, target, blocks, factor):
    owner, partner = [(jnp.arange(result.shape[axis_at]) // (result.shape[axis_at] // blocks)).reshape([-1 if axis == axis_at else 1 for axis in range(result.ndim)]) for axis_at in (source, target)]
    chosen = jax.random.permutation(key, blocks)[partner]
    strong = (owner == chosen) | (owner == (partner + blocks // 2) % blocks)
    return jnp.where(strong, factor * result, result)


def block_scale(rng, shape, split, least, high):
    def one(axis_at, shards_of):
        heights = jax.random.uniform(jax.random.fold_in(jax.random.fold_in(rng, 6), axis_at), (shards_of,), jnp.float32, least / len(split), high / len(split))
        return jnp.repeat(jnp.exp(heights), shape[axis_at] // shards_of).reshape((-1,) + (1,) * (len(shape) - axis_at - 1))

    gain = one(*split[0])
    for cut in split[1:]:
        gain = gain * one(*cut)
    return gain


def heavy_noise(rng, dims, deviation, most, shards, heavy, held_as=jnp.bfloat16):
    array = deviation * jax.random.normal(rng, dims, jnp.float32)
    if shards:
        array = array * block_scale(rng, dims, shards, -0.22, 0.18)
    return jnp.clip(raised(array, jax.random.fold_in(rng, 3), *heavy), -most, most).astype(held_as)


def setup_inputs(seed: int = 0) -> dict:
    keys = jax.random.split(jax.random.key(seed), 5)
    return {
        "tokens_in": heavy_noise(keys[0], (TOKENS, D), 1.0, 6.0, ((0, 16), (1, 16)), (0, 1, 16, 2.0)),
        "w_in": heavy_noise(keys[1], (D, FF), D ** -0.5, 0.15625, ((0, 2), (1, 16)), (1, 0, 16, 2.0)),
        "w_out": heavy_noise(keys[2], (D, FF), FF ** -0.5, 0.078125, ((0, 2), (1, 16)), (1, 0, 16, 2.0)),
        "grad_out": heavy_noise(keys[3], (TOKENS, D), 0.5, 3.0, ((0, 16), (1, 16)), (0, 1, 16, 2.0)),
    }


def gelu_tanh(value):
    return jax.nn.gelu(value, approximate=True)

def block_sum(left, right, parts):
    width = left.shape[1] // parts

    def step(total, index):
        start = (index * width).astype(jnp.int32)
        left_blk = lax.dynamic_slice_in_dim(left, start, width, 1)
        right_blk = lax.dynamic_slice_in_dim(right, start, width, 1)
        term = lax.dot_general(left_blk, right_blk, (((1,), (1,)), ((), ())), preferred_element_type=jnp.float32)
        term = lax.optimization_barrier(term.astype(jnp.bfloat16)).astype(jnp.float32)
        return (total + term, None)
    init = jnp.zeros((left.shape[0], right.shape[0]), jnp.float32)
    total, _ = lax.scan(step, init, jnp.arange(parts, dtype=jnp.int32))
    return total

def token_sum(left, right, blocks):
    height = left.shape[0] // blocks

    def step(total, index):
        start = (index * height).astype(jnp.int32)
        left_blk = lax.dynamic_slice_in_dim(left, start, height, 0)
        right_blk = lax.dynamic_slice_in_dim(right, start, height, 0)
        term = lax.dot_general(left_blk, right_blk, (((0,), (0,)), ((), ())), preferred_element_type=jnp.float32)
        term = lax.optimization_barrier(term.astype(jnp.bfloat16)).astype(jnp.float32)
        return (total + term, None)
    init = jnp.zeros((left.shape[1], right.shape[1]), jnp.float32)
    total, _ = lax.scan(step, init, jnp.arange(blocks, dtype=jnp.int32))
    return total

def reference(tokens_in, w_in, w_out, grad_out):
    pre = jnp.dot(tokens_in, w_in, preferred_element_type=jnp.float32)
    hidden = gelu_tanh(pre).astype(jnp.bfloat16)
    block_out = block_sum(hidden, w_out, N_COL).astype(jnp.bfloat16)
    grad_hidden = jnp.dot(grad_out, w_out, preferred_element_type=jnp.float32)
    _, pullback = jax.vjp(gelu_tanh, pre)
    grad_pre = pullback(grad_hidden)[0].astype(jnp.bfloat16)
    grad_tokens = block_sum(grad_pre, w_in, N_COL).astype(jnp.bfloat16)
    blocks = N_ROW * N_DEPTH
    grad_w_in = token_sum(tokens_in, grad_pre, blocks).astype(jnp.bfloat16)
    grad_w_out = token_sum(grad_out, hidden, blocks).astype(jnp.bfloat16)
    return (block_out, grad_tokens, grad_w_in, grad_w_out)
```

```python
import functools

import jax
import jax.numpy as jnp
from jax import lax
from jax.experimental import pallas as pl
from jax.experimental.pallas import tpu as pltpu
from jax.sharding import PartitionSpec as P

MESH = pl.DeviceIdType.MESH
F32 = jnp.float32
BF16 = jnp.bfloat16
C0 = 0.7978845608028654
C1 = 0.044715


def nt(left, right):
    return lax.dot_general(left, right, (((1,), (1,)), ((), ())), preferred_element_type=F32)


def nn(left, right):
    return jnp.dot(left, right, preferred_element_type=F32)


class Copies:
    def __init__(self, send, recv):
        self.send, self.recv, self.count, self.sent = send, recv, 0, []

    def make(self, src, dst, device):
        k = self.count
        self.count += 1
        return pltpu.make_async_remote_copy(
            src_ref=src,
            dst_ref=dst,
            send_sem=self.send.at[k],
            recv_sem=self.recv.at[k],
            device_id=device,
            device_id_type=MESH,
        )

    def start(self, src, dst, device):
        copy = self.make(src, dst, device)
        copy.start()
        self.sent.append(copy)
        return copy


def kernel(
    tok_ref, grd_ref, win_ref, wout_ref,
    outT_ref, gtokT_ref, gwin_ref, gwout_ref,
    acts, wbuf, wt, acc, dgel, hid, gpre, terms, wpart, sib, zrecv, zsend,
    rs1, ssum, rs2, send_sem, recv_sem, w_sem, bulk_send, bulk_recv,
):
    R, T = outT_ref.shape
    H = win_ref.shape[1]
    G = 4 * R
    row, col, z = lax.axis_index("row"), lax.axis_index("col"), lax.axis_index("depth")
    y, x = lax.div(col, 4), lax.rem(col, 4)
    other = 1 - row

    def at(yy, xx):
        return lax.rem(yy + 4, 4) * 4 + lax.rem(xx + 4, 4)

    p_plus = (row, at(y + row, x + other), z)
    p_minus = (row, at(y - row, x - other), z)
    q_plus = (row, at(y + other, x + row), z)
    q_minus = (row, at(y - other, x - row), z)
    z_plus = (row, col, lax.rem(z + 1, 8))
    z_minus = (row, col, lax.rem(z + 7, 8))
    sibling = (other, col, z)
    partners = (p_plus, p_minus, q_plus, q_minus, z_plus, z_minus, sibling)

    def slot_of(block, core):
        dy = lax.rem(lax.div(block, 4) - y + 4, 4)
        dx = lax.rem(lax.rem(block, 4) - x + 4, 4)
        return dy * (4 - 3 * core) + dx * (1 + 3 * core)

    def rows_of(block, core):
        return pl.ds(pl.multiple_of(slot_of(block, core) * R, 32), R)

    copies = Copies(send_sem, recv_sem)

    local = []
    for w, src in ((0, win_ref), (1, wout_ref)):
        for i in range(8):
            block = row * 8 + i
            cp = pltpu.make_async_copy(
                src.at[pl.ds(i * R, R)], wbuf.at[w, rows_of(block, row)], w_sem.at[w]
            )
            cp.start()

    acts[0, 0:R, :] = tok_ref[...].astype(F32).T.astype(BF16)
    acts[1, 0:R, :] = grd_ref[...].astype(F32).T.astype(BF16)

    barrier = pltpu.get_barrier_semaphore()
    for dev in partners:
        pl.semaphore_signal(barrier, inc=1, device_id=dev, device_id_type=MESH)
    pl.semaphore_wait(barrier, len(partners))

    def shard(a, g, j, lo=0, hi=None):
        hi = R if hi is None else hi
        return acts.at[a, pl.ds((g * 4 + j) * R + lo, hi - lo)]

    got = {}
    half = R // 2

    def to_p(a):
        got[a, 0, 3] = [copies.start(shard(a, 0, 0), shard(a, 0, 3), p_plus)]
        got[a, 0, 1] = [copies.start(shard(a, 0, 0), shard(a, 0, 1), p_minus)]

    def to_q(a, j):
        got[a, 3, j] = [copies.start(shard(a, 0, j), shard(a, 3, j), q_plus)]
        got[a, 1, j] = [copies.start(shard(a, 0, j), shard(a, 1, j), q_minus)]

    def need(a, g, j):
        for cp in got.get((a, g, j), []):
            cp.wait_recv()
        got[a, g, j] = []

    def p_forward(a):
        need(a, 0, 3)
        first = copies.start(shard(a, 0, 3, 0, half), shard(a, 0, 2, 0, half), p_plus)
        to_q(a, 3)
        need(a, 0, 1)
        second = copies.start(shard(a, 0, 1, half, R), shard(a, 0, 2, half, R), p_minus)
        to_q(a, 1)
        got[a, 0, 2] = [first, second]

    def p_last(a):
        need(a, 0, 2)
        to_q(a, 2)

    def q_forward(a, step):
        j, k = (0, 2) if step == 0 else (1, 3)
        if step == 0:
            j, k = 0, 3
        else:
            j, k = 1, 2
        need(a, 3, j)
        got[a, 2, j] = [copies.start(shard(a, 3, j), shard(a, 2, j), q_plus)]
        need(a, 1, k)
        got[a, 2, k] = [copies.start(shard(a, 1, k), shard(a, 2, k), q_minus)]

    def group(a, g):
        for j in range(4):
            need(a, g, j)

    to_p(0)
    to_q(0, 0)
    for w, src in ((0, win_ref), (1, wout_ref)):
        for i in range(8):
            block = row * 8 + i
            pltpu.make_async_remote_copy(
                src_ref=src.at[pl.ds(i * R, R)],
                dst_ref=wbuf.at[w, rows_of(block, other)],
                send_sem=bulk_send.at[w],
                recv_sem=bulk_recv.at[w],
                device_id=sibling,
                device_id_type=MESH,
            ).start()
    to_p(1)
    p_forward(0)
    to_q(1, 0)
    p_last(0)

    def weights(w, src):
        pltpu.make_async_copy(src, wbuf.at[w, pl.ds(0, 8 * R)], w_sem.at[w]).wait()
        pltpu.make_async_remote_copy(
            src_ref=src, dst_ref=wbuf.at[w, pl.ds(0, 8 * R)], send_sem=bulk_send.at[w],
            recv_sem=bulk_recv.at[w], device_id=sibling, device_id_type=MESH,
        ).wait()

        @pl.loop(0, 4)
        def _(g):
            wt[w, g] = wbuf[w, pl.ds(pl.multiple_of(g * G, 128), G), :].T

    weights(0, win_ref)
    p_forward(1)
    p_last(1)
    q_forward(0, 0)
    q_forward(0, 1)
    weights(1, wout_ref)

    def project(a):
        for n, g in enumerate((0, 3, 1, 2)):
            group(a, g)
            part = nn(wt[a, g], acts[a, pl.ds(g * G, G), :])
            if n == 0:
                acc[...] = part
            else:
                acc[...] += part

    project(0)
    q_forward(1, 0)

    step = 32

    @pl.loop(0, H // step)
    def _(i):
        rows = pl.ds(pl.multiple_of(i * step, step), step)
        v = acc[rows, :]
        sq = v * v
        t = jnp.tanh(C0 * (v + C1 * (sq * v)))
        cdf = 0.5 * (1.0 + t)
        hid[rows, :] = (v * cdf).astype(BF16)
        dgel[rows, :] = cdf + (0.5 * C0) * v * (1.0 - t * t) * (1.0 + (3.0 * C1) * sq)

    q_forward(1, 1)

    def make_terms(a, w, src):
        @pl.loop(0, 4)
        def _(g):
            rows = pl.ds(pl.multiple_of(g * G, 128), G)
            terms[a, rows, :] = nn(wbuf[w, rows, :], src[...]).astype(BF16)

    def make_wpart(b, a, src):
        @pl.loop(0, 4)
        def _(g):
            rows = pl.ds(pl.multiple_of(g * G, 128), G)
            wpart[b, rows, :] = nt(acts[a, rows, :], src[...]).astype(BF16)

    def add(dst, srcs, rows, out=BF16):
        block = 32 if rows % 32 == 0 else 16

        @pl.loop(0, rows // block)
        def _(i):
            here = pl.multiple_of(i * block, block)
            total = None
            for ref, off in srcs:
                part = ref[pl.ds(pl.multiple_of(off + here, 16), block), :].astype(F32)
                total = part if total is None else total + part
            ref, off = dst
            ref[pl.ds(pl.multiple_of(off + here, 16), block), :] = total.astype(out)

    rs = {}

    def rs1a(a):
        t = terms.at[a]
        r = rs1.at[a]
        rs[a, "ra"] = copies.start(t.at[pl.ds(8 * R, 2 * R)], r.at[pl.ds(0, 2 * R)], q_plus)
        rs[a, "rb"] = copies.start(t.at[pl.ds(10 * R, 2 * R)], r.at[pl.ds(2 * R, 2 * R)], q_minus)
        rs[a, "rc1"] = copies.start(t.at[pl.ds(6 * R, 2 * R)], r.at[pl.ds(6 * R, 2 * R)], q_plus)
        rs[a, "rd0"] = copies.start(t.at[pl.ds(12 * R, 2 * R)], r.at[pl.ds(8 * R, 2 * R)], q_minus)

    def rs1b(a):
        t = terms.at[a]
        r = rs1.at[a]
        rs[a, "ra"].wait_recv()
        add((t, 4 * R), ((t, 4 * R), (r, 0)), 2 * R)
        rs[a, "rc0"] = copies.start(t.at[pl.ds(4 * R, 2 * R)], r.at[pl.ds(4 * R, 2 * R)], q_plus)
        rs[a, "rb"].wait_recv()
        add((t, 14 * R), ((t, 14 * R), (r, 2 * R)), 2 * R)
        rs[a, "rd1"] = copies.start(t.at[pl.ds(14 * R, 2 * R)], r.at[pl.ds(10 * R, 2 * R)], q_minus)

    def rs1c(a):
        t = terms.at[a]
        r = rs1.at[a]
        s = ssum.at[a]
        e = rs2.at[a]
        rs[a, "rc1"].wait_recv()
        rs[a, "rd1"].wait_recv()
        add((s, 2 * R), ((t, 2 * R), (r, 6 * R), (r, 10 * R)), 2 * R)
        rs[a, "re"] = copies.start(s.at[pl.ds(2 * R, half)], e.at[pl.ds(0, half)], p_plus)
        rs[a, "rf"] = copies.start(s.at[pl.ds(2 * R + half, half)], e.at[pl.ds(half, half)], p_minus)
        rs[a, "rc0"].wait_recv()
        rs[a, "rd0"].wait_recv()
        add((s, R), ((t, R), (r, 5 * R), (r, 9 * R)), R)

    def rs2b(a):
        s = ssum.at[a]
        e = rs2.at[a]
        rs[a, "re"].wait_recv()
        add((s, R), ((s, R), (e, 0)), half)
        rs[a, "rg"] = copies.start(s.at[pl.ds(R, R)], e.at[pl.ds(R, R)], p_plus)
        rs[a, "rf"].wait_recv()
        add((s, 3 * R + half), ((s, 3 * R + half), (e, half)), half)
        rs[a, "rh"] = copies.start(s.at[pl.ds(3 * R, R)], e.at[pl.ds(2 * R, R)], p_minus)

    def rs2c(a, out):
        t = terms.at[a]
        r = rs1.at[a]
        e = rs2.at[a]
        rs[a, "rg"].wait_recv()
        rs[a, "rh"].wait_recv()
        add((out, 0), ((t, 0), (r, 4 * R), (r, 8 * R), (e, R), (e, 2 * R)), R)

    finals = (gwout_ref, gwin_ref)
    zs = {}
    signs = (1, -1)
    orders = [(4 * d, -3 * d, 3 * d, -2 * d, 2 * d, -d, d, 0) for d in signs]

    def chunk(delta):
        return lax.rem(z + delta + 8, 8)

    def sib_send(b):
        for n, delta in enumerate(orders[b]):
            block = other * 8 + chunk(delta)
            zs[b, "sib", delta] = copies.start(
                wpart.at[b, rows_of(block, row)], sib.at[b, pl.ds(n * R, R)], sibling
            )

    def own(b, delta):
        zs[b, "sib", delta].wait_recv()
        n = orders[b].index(delta)
        mine = slot_of(row * 8 + chunk(delta), row) * R
        return ((wpart.at[b], mine), (sib.at[b], n * R))

    def ends(b, long):
        forward = (signs[b] > 0) == long
        return z_plus if forward else z_minus

    def z_step(b, long, s):
        hops, base = (4, 0) if long else (3, 4)
        delta = signs[b] * (4 - s) if long else -signs[b] * (3 - s)
        srcs = own(b, delta)
        if s > 0:
            zs[b, long, s - 1].wait_recv()
            srcs += ((zrecv.at[b], (base + s - 1) * R),)
        add((zsend.at[b], (base + s) * R), srcs, R)
        zs[b, long, s] = copies.start(
            zsend.at[b, pl.ds((base + s) * R, R)], zrecv.at[b, pl.ds((base + s) * R, R)], ends(b, long)
        )

    def z_both(b, s):
        z_step(b, True, s)
        if s < 3:
            z_step(b, False, s)

    def place(b, delta):
        return finals[b].at[pl.ds(pl.multiple_of(chunk(delta) * R, 32), R)]

    def z_final(b):
        srcs = own(b, 0)
        zs[b, True, 3].wait_recv()
        zs[b, False, 2].wait_recv()
        srcs += ((zrecv.at[b], 3 * R), (zrecv.at[b], 6 * R))
        add((zsend.at[b], 7 * R), srcs, R)
        mine = zsend.at[b, pl.ds(7 * R, R)]
        for long in (True, False):
            zs[b, "ag", long, 0] = copies.start(mine, place(b, 0), ends(b, long))
        zs[b, "own"] = pltpu.make_async_copy(mine, place(b, 0), w_sem.at[2 + b])
        zs[b, "own"].start()

    def z_gather(b, s):
        for long in (True, False):
            if s >= (4 if long else 3):
                continue
            delta = (-signs[b] if long else signs[b]) * s
            zs[b, "ag", long, s - 1].wait_recv()
            zs[b, "ag", long, s] = copies.start(place(b, delta), place(b, delta), ends(b, long))

    def z_end(b):
        zs[b, "own"].wait()
        zs[b, "ag", True, 3].wait_recv()
        zs[b, "ag", False, 2].wait_recv()

    make_terms(0, 1, hid)
    rs1a(0)
    for g in (0, 3, 1, 2):
        group(1, g)
    make_wpart(0, 1, hid)
    sib_send(0)
    project(1)
    z_both(0, 0)

    @pl.loop(0, H // step)
    def _(i):
        rows = pl.ds(pl.multiple_of(i * step, step), step)
        gpre[rows, :] = (acc[rows, :] * dgel[rows, :]).astype(BF16)

    make_wpart(1, 0, gpre)
    sib_send(1)
    rs1b(0)
    make_terms(1, 0, gpre)
    rs1a(1)
    z_both(1, 0)
    z_both(0, 1)
    rs1c(0)
    z_both(1, 1)
    z_both(0, 2)
    rs1b(1)
    rs2b(0)
    z_both(1, 2)
    z_both(0, 3)
    rs1c(1)
    rs2c(0, outT_ref)
    z_both(1, 3)
    z_final(0)
    rs2b(1)
    z_final(1)
    z_gather(0, 1)
    rs2c(1, gtokT_ref)
    z_gather(1, 1)
    z_gather(0, 2)
    z_gather(1, 2)
    z_gather(0, 3)
    z_gather(1, 3)
    z_end(0)
    z_end(1)
    for cp in copies.sent:
        cp.wait_send()


N_COPIES = 2 * 16 + 2 * 10 + 2 * (8 + 7 + 7)


def body(tokens_in, w_in, w_out, grad_out):
    T, R = tokens_in.shape
    H = w_in.shape[1]
    vmem = pl.BlockSpec(memory_space=pltpu.VMEM)
    hbm = pl.BlockSpec(memory_space=pl.ANY)
    outT, gtokT, g_in, g_out = pl.pallas_call(
        kernel,
        out_shape=(
            jax.ShapeDtypeStruct((R, T), BF16),
            jax.ShapeDtypeStruct((R, T), BF16),
            jax.ShapeDtypeStruct(w_in.shape, BF16),
            jax.ShapeDtypeStruct(w_out.shape, BF16),
        ),
        in_specs=[vmem, vmem, hbm, hbm],
        out_specs=(vmem, vmem, hbm, hbm),
        scratch_shapes=[
            pltpu.VMEM((2, 16 * R, T), BF16),
            pltpu.VMEM((2, 16 * R, H), BF16),
            pltpu.VMEM((2, 4, H, 4 * R), BF16),
            pltpu.VMEM((H, T), F32),
            pltpu.VMEM((H, T), F32),
            pltpu.VMEM((H, T), BF16),
            pltpu.VMEM((H, T), BF16),
            pltpu.VMEM((2, 16 * R, T), BF16),
            pltpu.VMEM((2, 16 * R, H), BF16),
            pltpu.VMEM((2, 8 * R, H), BF16),
            pltpu.VMEM((2, 7 * R, H), BF16),
            pltpu.VMEM((2, 8 * R, H), BF16),
            pltpu.VMEM((2, 12 * R, T), BF16),
            pltpu.VMEM((2, 4 * R, T), BF16),
            pltpu.VMEM((2, 3 * R, T), BF16),
            pltpu.SemaphoreType.DMA((N_COPIES,)),
            pltpu.SemaphoreType.DMA((N_COPIES,)),
            pltpu.SemaphoreType.DMA((4,)),
            pltpu.SemaphoreType.DMA((2,)),
            pltpu.SemaphoreType.DMA((2,)),
        ],
        compiler_params=pltpu.CompilerParams(
            collective_id=0, has_side_effects=True, vmem_limit_bytes=63 * 1024 * 1024
        ),
    )(tokens_in, grad_out, w_in, w_out)
    return outT.T, gtokT.T, g_in, g_out


def solution(mesh):
    placed = P(("row", "depth"), "col")
    weights = P("row", "col")
    return jax.shard_map(
        body,
        mesh=mesh,
        in_specs=(placed, weights, weights, placed),
        out_specs=(placed, placed, weights, weights),
        check_vma=False,
    )
```

```python
import functools

import jax
import jax.numpy as jnp
from jax import lax
from jax.experimental import pallas as pl
from jax.experimental.pallas import tpu as pltpu
from jax.sharding import PartitionSpec as P

MESH = pl.DeviceIdType.MESH
F32 = jnp.float32
BF16 = jnp.bfloat16
C0 = 0.7978845608028654
C1 = 0.044715


def nt(left, right):
    return lax.dot_general(left, right, (((1,), (1,)), ((), ())), preferred_element_type=F32)


def nn(left, right):
    return jnp.dot(left, right, preferred_element_type=F32)


class Local:
    def __init__(self, copy):
        self.wait_recv = copy.wait


class Copies:
    def __init__(self, send, recv):
        self.send, self.recv, self.count, self.sent = send, recv, 0, []

    def make(self, src, dst, device):
        k = self.count
        self.count += 1
        return pltpu.make_async_remote_copy(
            src_ref=src,
            dst_ref=dst,
            send_sem=self.send.at[k],
            recv_sem=self.recv.at[k],
            device_id=device,
            device_id_type=MESH,
        )

    def start(self, src, dst, device):
        copy = self.make(src, dst, device)
        copy.start()
        self.sent.append(copy)
        return copy


ORDER = (
    ((0, 0), (0, 1), (0, 3), (1, 0)),
    ((3, 0), (1, 1), (1, 3), (3, 1)),
    ((3, 3), (0, 2), (2, 0), (1, 2)),
    ((3, 2), (2, 1), (2, 3), (2, 2)),
)
FLAT = [pair for group in ORDER for pair in group]
SLOT = {pair: n for n, pair in enumerate(FLAT)}


def kernel(
    tok_ref, grd_ref, win_ref, wout_ref,
    outT_ref, gtokT_ref, gwin_ref, gwout_ref,
    acts, wbuf, wt, acc, dgel, hid, gpre, terms, wpart, sib, zrecv, fin,
    rs1, ssum, rs2, send_sem, recv_sem, w_sem, bulk_send, bulk_recv, o_sem, o_send, o_recv,
):
    R, T = outT_ref.shape
    H = win_ref.shape[1]
    G = 4 * R
    half = R // 2
    row, col, z = lax.axis_index("row"), lax.axis_index("col"), lax.axis_index("depth")
    y, x = lax.div(col, 4), lax.rem(col, 4)
    other = 1 - row

    def at(yy, xx):
        return lax.rem(yy + 4, 4) * 4 + lax.rem(xx + 4, 4)

    p_plus = (row, at(y + row, x + other), z)
    p_minus = (row, at(y - row, x - other), z)
    q_plus = (row, at(y + other, x + row), z)
    q_minus = (row, at(y - other, x - row), z)
    z_plus = (row, col, lax.rem(z + 1, 8))
    z_minus = (row, col, lax.rem(z + 7, 8))
    sibling = (other, col, z)
    partners = (p_plus, p_minus, q_plus, q_minus, z_plus, z_minus, sibling)

    barrier = pltpu.get_barrier_semaphore()
    for dev in partners:
        pl.semaphore_signal(barrier, inc=1, device_id=dev, device_id_type=MESH)

    copies = Copies(send_sem, recv_sem)
    owns = [
        pltpu.make_async_copy(src, acts.at[a, pl.ds(0, R)], w_sem.at[2 + a])
        for a, src in ((0, tok_ref), (1, grd_ref))
    ]
    for cp in owns:
        cp.start()

    def offset(g, j):
        one, two = SLOT[g, j], SLOT[j, g]
        if one == two:
            return one * R
        return pl.multiple_of((one + row * (two - one)) * R, 32)

    def shard(a, g, j, lo=0, hi=None):
        hi = R if hi is None else hi
        start = offset(g, j) + lo
        if not isinstance(start, int):
            start = pl.multiple_of(start, 16)
        return acts.at[a, pl.ds(start, hi - lo)]

    got = {}

    local = [Local(cp) for cp in owns]
    got.update({(0, 0, 0): [local[0]], (1, 0, 0): [local[1]]})

    def came(a, g, j, copy):
        got.setdefault((a, g, j), []).append(copy)

    def need(a, g, j):
        for cp in got.pop((a, g, j), []):
            cp.wait_recv()

    def to_p(a):
        src = (tok_ref, grd_ref)[a]
        came(a, 0, 3, copies.start(src, shard(a, 0, 3), p_plus))
        came(a, 0, 1, copies.start(src, shard(a, 0, 1), p_minus))

    def to_q(a, j):
        if j:
            need(a, 0, j)
        src = (tok_ref, grd_ref)[a] if j == 0 else shard(a, 0, j)
        came(a, 3, j, copies.start(src, shard(a, 3, j), q_plus))
        came(a, 1, j, copies.start(src, shard(a, 1, j), q_minus))

    def pf(a, g):
        need(a, 0, g)
        lo, hi, dev = (0, half, p_plus) if g == 3 else (half, R, p_minus)
        came(a, 0, 2, copies.start(shard(a, 0, g, lo, hi), shard(a, 0, 2, lo, hi), dev))

    def qf(a, g, j):
        need(a, g, j)
        came(a, 2, j, copies.start(shard(a, g, j), shard(a, 2, j), q_plus if g == 3 else q_minus))

    def group(a, n):
        if n == 0:
            need(a, 0, 0)
        for dy, dx in ORDER[n]:
            need(a, dy, dx)
            need(a, dx, dy)

    pl.semaphore_wait(barrier, len(partners))
    def wload():
        for dy in range(4):
            place_weights(dy)

    def place_weights(dy):
        yy = lax.rem(y + dy, 4)

        @pl.when(lax.div(yy, 2) == row)
        def _():
            for dx in range(4):
                n = SLOT[dy, dx]
                start = ((yy - 2 * row) * 4 + lax.rem(x + dx, 4)) * R
                block = pl.ds(pl.multiple_of(start, 32), R)
                for w, src in ((0, win_ref), (1, wout_ref)):
                    there = wbuf.at[w, pl.ds(n * R, R)]
                    pltpu.make_async_copy(src.at[block], there, w_sem.at[w]).start()
                    pltpu.make_async_remote_copy(
                        src_ref=src.at[block], dst_ref=there, send_sem=bulk_send.at[w],
                        recv_sem=bulk_recv.at[w], device_id=sibling, device_id_type=MESH,
                    ).start()

    def trans(w):
        src = (win_ref, wout_ref)[w]
        pltpu.make_async_copy(src, wbuf.at[w, pl.ds(0, 8 * R)], w_sem.at[w]).wait()
        pltpu.make_async_remote_copy(
            src_ref=src, dst_ref=wbuf.at[w, pl.ds(0, 8 * R)], send_sem=bulk_send.at[w],
            recv_sem=bulk_recv.at[w], device_id=sibling, device_id_type=MESH,
        ).wait()

        @pl.loop(0, 4)
        def _(g):
            wt[w, g] = wbuf[w, pl.ds(pl.multiple_of(g * G, 128), G), :].T

    def project(a, n):
        group(a, n)
        part = nn(wt[a, n], acts[a, pl.ds(n * G, G), :])
        if n == 0:
            acc[...] = part
        else:
            acc[...] += part

    def rows_at(n):
        return pl.ds(n * G if isinstance(n, int) else pl.multiple_of(n * G, 128), G)

    def make_terms(a, w, src, n):
        rows = rows_at(n)
        terms[a, rows, :] = nn(wbuf[w, rows, :], src[...]).astype(BF16)

    def make_wpart(b, a, src, n):
        rows = rows_at(n)
        wpart[b, rows, :] = nt(acts[a, rows, :], src[...]).astype(BF16)

    def add(dst, srcs, rows, out=BF16):
        block = 32 if rows % 32 == 0 else 16

        @pl.loop(0, rows // block)
        def _(i):
            here = pl.multiple_of(i * block, block)
            total = None
            for ref, off in srcs:
                part = ref[pl.ds(pl.multiple_of(off + here, 16), block), :].astype(F32)
                total = part if total is None else total + part
            ref, off = dst
            ref[pl.ds(pl.multiple_of(off + here, 16), block), :] = total.astype(out)

    rs = {}

    def piece(ref, start, rows):
        if not isinstance(start, int):
            start = pl.multiple_of(start, 16)
        return ref.at[pl.ds(start, rows)]

    def rs_a(a, g, j):
        t, r = terms.at[a], rs1.at[a]
        base, dev = {1: (4, q_plus), 3: (8, q_minus)}.get(g, (0, q_plus if j < 2 else q_minus))
        key = {1: "rc", 3: "rd"}.get(g, "ra")
        rs[a, key, j] = copies.start(piece(t, offset(g, j), R), piece(r, (base + j) * R, R), dev)

    def rs_b(a, g, j):
        t, r = terms.at[a], rs1.at[a]
        rs[a, "ra", j].wait_recv()
        add((t, offset(g, j)), ((t, offset(g, j)), (r, j * R)), R)
        rs_a(a, g, j)

    def rs_c(a, j):
        t, r, s, e = terms.at[a], rs1.at[a], ssum.at[a], rs2.at[a]
        rs[a, "rc", j].wait_recv()
        rs[a, "rd", j].wait_recv()
        add((s, j * R), ((t, offset(0, j)), (r, (4 + j) * R), (r, (8 + j) * R)), R)
        if j == 2:
            rs[a, "re"] = copies.start(piece(s, 2 * R, half), piece(e, 0, half), p_plus)
            rs[a, "rf"] = copies.start(piece(s, 2 * R + half, half), piece(e, half, half), p_minus)

    def rs_d(a, j):
        s, e = ssum.at[a], rs2.at[a]
        lo, key, dev = (0, "re", p_plus) if j == 1 else (half, "rf", p_minus)
        rs[a, key].wait_recv()
        add((s, j * R + lo), ((s, j * R + lo), (e, lo)), half)
        rs[a, "last", j] = copies.start(piece(s, j * R, R), piece(e, (1 + j // 2) * R, R), dev)

    def rs_e(a):
        t, r, e, out = terms.at[a], rs1.at[a], rs2.at[a], (outT_ref, gtokT_ref)[a]
        rs[a, "rc", 0].wait_recv()
        rs[a, "rd", 0].wait_recv()
        rs[a, "last", 1].wait_recv()
        rs[a, "last", 3].wait_recv()
        add((out, 0), ((t, 0), (r, 4 * R), (r, 8 * R), (e, R), (e, 2 * R)), R)

    finals = (gwout_ref, gwin_ref)
    zs = {}

    def sign(h):
        return 1 - 2 * h

    def order(h):
        d = sign(h)
        return (4 * d, -3 * d, 3 * d, -2 * d, 2 * d, -d, d, 0)

    def chunk(delta):
        return lax.rem(z + delta + 8, 8)

    def sib_send(b, h):
        for n, delta in enumerate(order(h)):
            start = h * 8 * R + other * G + chunk(delta) * half
            zs[b, h, "sib", delta] = copies.start(
                piece(wpart.at[b], start, half), piece(sib.at[b], h * G + n * half, half), sibling
            )

    def own(b, h, delta):
        zs[b, h, "sib", delta].wait_recv()
        n = order(h).index(delta)
        mine = pl.multiple_of(h * 8 * R + row * G + chunk(delta) * half, 16)
        return ((wpart.at[b], mine), (sib.at[b], h * G + n * half))

    def ends(h, long):
        return z_plus if (sign(h) > 0) == long else z_minus

    def z_one(b, h, long, n):
        base = h * 7 + (0 if long else 4)
        delta = sign(h) * (4 - n) if long else -sign(h) * (3 - n)
        srcs = own(b, h, delta)
        if n > 0:
            zs[b, h, long, n - 1].wait_recv()
            srcs += ((zrecv.at[b], (base + n - 1) * half),)
        add(srcs[0], srcs, half)
        zs[b, h, long, n] = copies.start(
            piece(*srcs[0], half), piece(zrecv.at[b], (base + n) * half, half), ends(h, long)
        )

    def place(b, h, delta):
        return piece(fin.at[b], h * G + chunk(delta) * half, half)

    def z_final(b, h):
        srcs = own(b, h, 0)
        zs[b, h, True, 3].wait_recv()
        zs[b, h, False, 2].wait_recv()
        base = h * 7
        srcs += ((zrecv.at[b], (base + 3) * half), (zrecv.at[b], (base + 6) * half))
        add((fin.at[b], pl.multiple_of(h * G + chunk(0) * half, 16)), srcs, half)
        for long in (True, False):
            zs[b, h, "ag", long, 0] = copies.start(place(b, h, 0), place(b, h, 0), ends(h, long))

    def z_gather(b, h, long, n):
        delta = (-sign(h) if long else sign(h)) * n
        zs[b, h, "ag", long, n - 1].wait_recv()
        zs[b, h, "ag", long, n] = copies.start(place(b, h, delta), place(b, h, delta), ends(h, long))

    def owner_of(h, j, core):
        one, two = FLAT[h * 8 + j], FLAT[h * 8 + 4 + j]
        dy, dx = (p + core * (q - p) for p, q in zip(one, two))
        yy = lax.rem(y + dy, 4)
        target = lax.div(yy, 2)
        start = ((yy - 2 * target) * 4 + lax.rem(x + dx, 4)) * R
        return target, pl.ds(pl.multiple_of(start, 32), R)

    def out_here(b, h, j, rows):
        n = (b * 2 + h) * 4 + j
        return pltpu.make_async_copy(piece(fin.at[b], h * G + j * R, R), finals[b].at[rows], o_sem.at[n])

    def out_there(b, h, j, rows):
        n = (b * 2 + h) * 4 + j
        return pltpu.make_async_remote_copy(
            src_ref=piece(fin.at[b], h * G + j * R, R), dst_ref=finals[b].at[rows],
            send_sem=o_send.at[n], recv_sem=o_recv.at[n], device_id=sibling, device_id_type=MESH,
        )

    def z_end(b, h):
        zs[b, h, "ag", True, 3].wait_recv()
        zs[b, h, "ag", False, 2].wait_recv()
        for j in range(4):
            target, rows = owner_of(h, j, row)
            pl.when(target == row)(lambda: out_here(b, h, j, rows).start())
            pl.when(target != row)(lambda: out_there(b, h, j, rows).start())

    def z_stored(b, h):
        for j in range(4):
            target, rows = owner_of(h, j, row)
            pl.when(target == row)(lambda: out_here(b, h, j, rows).wait())
            pl.when(target != row)(lambda: out_there(b, h, j, rows).wait_send())
            target, rows = owner_of(h, j, other)
            pl.when(target == row)(lambda: out_there(b, h, j, rows).wait_recv())

    def gelu():
        step = 32

        @pl.loop(0, H // step)
        def _(i):
            rows = pl.ds(pl.multiple_of(i * step, step), step)
            v = acc[rows, :]
            sq = v * v
            t = jnp.tanh(C0 * (v + C1 * (sq * v)))
            cdf = 0.5 * (1.0 + t)
            hid[rows, :] = (v * cdf).astype(BF16)
            dgel[rows, :] = cdf + (0.5 * C0) * v * (1.0 - t * t) * (1.0 + (3.0 * C1) * sq)

    def gelu_back():
        step = 32

        @pl.loop(0, H // step)
        def _(i):
            rows = pl.ds(pl.multiple_of(i * step, step), step)
            gpre[rows, :] = (acc[rows, :] * dgel[rows, :]).astype(BF16)

    def wpart_o(b, h):
        if b == 0:
            group(1, 2 * h)
            group(1, 2 * h + 1)
        make_wpart(b, 1 - b, (hid, gpre)[b], 2 * h + other)

    def wpart_m(b, h):
        make_wpart(b, 1 - b, (hid, gpre)[b], 2 * h + row)

    def terms_of(a, n):
        make_terms(a, 1 - a, (hid, gpre)[a], n)

    to_p(0)
    to_q(0, 0)
    wload()
    pf(0, 3)
    pf(0, 1)
    to_q(0, 3)
    to_q(0, 1)
    to_p(1)
    to_q(1, 0)
    qf(0, 3, 0)
    trans(0)
    to_q(0, 2)
    project(0, 0)
    qf(0, 1, 3)
    trans(1)
    qf(0, 3, 1)
    project(0, 1)
    pf(1, 3)
    pf(1, 1)
    to_q(1, 3)
    to_q(1, 1)
    qf(1, 3, 0)
    qf(0, 1, 2)
    project(0, 2)
    to_q(1, 2)
    qf(1, 1, 3)
    qf(1, 3, 1)
    project(0, 3)
    gelu()
    wpart_o(0, 0)
    sib_send(0, 0)
    qf(1, 1, 2)
    wpart_m(0, 0)
    project(1, 0)
    project(1, 1)
    terms_of(0, 3)
    z_one(0, 0, True, 0)
    z_one(0, 0, False, 0)
    terms_of(0, 2)
    terms_of(0, 1)
    terms_of(0, 0)
    rs_a(0, 2, 3)
    rs_a(0, 2, 2)
    rs_a(0, 2, 1)
    rs_a(0, 2, 0)
    rs_a(0, 3, 1)
    wpart_o(0, 1)
    sib_send(0, 1)
    wpart_m(0, 1)
    project(1, 2)
    project(1, 3)
    gelu_back()
    z_one(0, 0, True, 1)
    z_one(0, 0, False, 1)
    z_one(0, 1, True, 0)
    z_one(0, 1, False, 0)
    wpart_o(1, 0)
    sib_send(1, 0)
    wpart_m(1, 0)
    wpart_o(1, 1)
    sib_send(1, 1)
    wpart_m(1, 1)
    rs_b(0, 3, 3)
    z_one(1, 0, True, 0)
    rs_b(0, 3, 2)
    z_one(1, 0, False, 0)
    rs_b(0, 1, 1)
    rs_b(0, 1, 0)
    rs_a(0, 3, 0)
    rs_a(0, 1, 3)
    rs_a(0, 1, 2)
    terms_of(1, 3)
    terms_of(1, 2)
    z_one(0, 0, True, 2)
    z_one(0, 0, False, 2)
    z_one(1, 1, True, 0)
    terms_of(1, 1)
    z_one(1, 1, False, 0)
    terms_of(1, 0)
    rs_a(1, 2, 3)
    rs_a(1, 2, 2)
    rs_a(1, 2, 1)
    rs_a(1, 2, 0)
    rs_a(1, 3, 1)
    rs_a(1, 3, 0)
    rs_a(1, 1, 3)
    rs_a(1, 1, 2)
    z_one(0, 1, False, 1)
    z_one(0, 1, True, 1)
    rs_c(0, 1)
    z_one(1, 0, True, 1)
    z_one(1, 0, False, 1)
    rs_c(0, 3)
    z_one(0, 0, True, 3)
    rs_b(1, 3, 3)
    rs_c(0, 2)
    z_one(1, 1, False, 1)
    z_one(1, 1, True, 1)
    rs_b(1, 3, 2)
    rs_b(1, 1, 1)
    z_one(0, 1, False, 2)
    z_one(0, 1, True, 2)
    rs_b(1, 1, 0)
    z_one(1, 0, True, 2)
    z_one(1, 0, False, 2)
    rs_c(1, 3)
    z_final(0, 0)
    z_one(1, 1, True, 2)
    rs_d(0, 3)
    rs_d(0, 1)
    rs_c(1, 2)
    z_one(1, 1, False, 2)
    z_one(0, 1, True, 3)
    rs_c(1, 1)
    rs_d(1, 3)
    rs_e(0)
    z_one(1, 0, True, 3)
    z_gather(0, 0, False, 1)
    rs_d(1, 1)
    z_gather(0, 0, True, 1)
    z_one(1, 1, True, 3)
    rs_e(1)
    z_final(0, 1)
    z_final(1, 0)
    z_gather(0, 0, False, 2)
    z_gather(0, 0, True, 2)
    z_final(1, 1)
    z_gather(0, 1, False, 1)
    z_gather(0, 1, True, 1)
    z_gather(1, 0, True, 1)
    z_gather(1, 0, False, 1)
    z_gather(0, 0, True, 3)
    z_gather(1, 1, False, 1)
    z_gather(1, 1, True, 1)
    z_gather(0, 1, False, 2)
    z_gather(0, 1, True, 2)
    z_gather(1, 0, True, 2)
    z_gather(1, 0, False, 2)
    z_end(0, 0)
    z_gather(1, 1, True, 2)
    z_gather(1, 1, False, 2)
    z_gather(0, 1, True, 3)
    z_stored(0, 0)
    z_gather(1, 0, True, 3)
    z_gather(1, 1, True, 3)
    z_end(0, 1)
    z_end(1, 0)
    z_end(1, 1)
    z_stored(0, 1)
    z_stored(1, 0)
    z_stored(1, 1)
    for cp in copies.sent:
        cp.wait_send()


def settle(*refs):
    srcs, dsts, held, (into, out) = refs[:4], refs[4:8], refs[8:12], refs[12:]
    moves = []
    for src, dst, via in zip(srcs, dsts, held):
        parts = 1 if src.shape[0] < 512 else 4
        rows = src.shape[0] // parts
        for i in range(parts):
            here = pl.ds(i * rows, rows)
            n = len(moves)
            moves.append(
                (
                    pltpu.make_async_copy(src.at[here], via.at[here], into.at[n]),
                    pltpu.make_async_copy(via.at[here], dst.at[here], out.at[n]),
                )
            )
    for first, _ in moves:
        first.start()
    for first, second in moves:
        first.wait()
        second.start()
    for _, second in moves:
        second.wait()


N_COPIES = 2 * 16 + 2 * 16 + 4 * (8 + 7 + 7)


def body(tokens_in, w_in, w_out, grad_out):
    T, R = tokens_in.shape
    H = w_in.shape[1]
    tokT, grdT = tokens_in.T, grad_out.T
    vmem = pl.BlockSpec(memory_space=pltpu.VMEM)
    hbm = pl.BlockSpec(memory_space=pl.ANY)
    outT, gtokT, g_in, g_out = pl.pallas_call(
        kernel,
        out_shape=(
            jax.ShapeDtypeStruct((R, T), BF16),
            jax.ShapeDtypeStruct((R, T), BF16),
            jax.ShapeDtypeStruct(w_in.shape, BF16),
            jax.ShapeDtypeStruct(w_out.shape, BF16),
        ),
        in_specs=[hbm] * 4,
        out_specs=(vmem, vmem, hbm, hbm),
        scratch_shapes=[
            pltpu.VMEM((2, 16 * R, T), BF16),
            pltpu.VMEM((2, 16 * R, H), BF16),
            pltpu.VMEM((2, 4, H, 4 * R), BF16),
            pltpu.VMEM((H, T), F32),
            pltpu.VMEM((H, T), F32),
            pltpu.VMEM((H, T), BF16),
            pltpu.VMEM((H, T), BF16),
            pltpu.VMEM((2, 16 * R, T), BF16),
            pltpu.VMEM((2, 16 * R, H), BF16),
            pltpu.VMEM((2, 8 * R, H), BF16),
            pltpu.VMEM((2, 7 * R, H), BF16),
            pltpu.VMEM((2, 8 * R, H), BF16),
            pltpu.VMEM((2, 12 * R, T), BF16),
            pltpu.VMEM((2, 4 * R, T), BF16),
            pltpu.VMEM((2, 3 * R, T), BF16),
            pltpu.SemaphoreType.DMA((N_COPIES,)),
            pltpu.SemaphoreType.DMA((N_COPIES,)),
            pltpu.SemaphoreType.DMA((4,)),
            pltpu.SemaphoreType.DMA((2,)),
            pltpu.SemaphoreType.DMA((2,)),
            pltpu.SemaphoreType.DMA((16,)),
            pltpu.SemaphoreType.DMA((16,)),
            pltpu.SemaphoreType.DMA((16,)),
        ],
        compiler_params=pltpu.CompilerParams(
            collective_id=0, has_side_effects=True, vmem_limit_bytes=63 * 1024 * 1024
        ),
    )(tokT, grdT, w_in, w_out)
    arrays = (outT, gtokT, g_in, g_out)
    outT, gtokT, g_in, g_out = pl.pallas_call(
        settle,
        out_shape=tuple(jax.ShapeDtypeStruct(a.shape, BF16) for a in arrays),
        in_specs=[hbm] * 4,
        out_specs=(hbm,) * 4,
        scratch_shapes=[pltpu.VMEM(a.shape, BF16) for a in arrays] + [pltpu.SemaphoreType.DMA((10,))] * 2,
    )(*arrays)
    return outT.T, gtokT.T, g_in, g_out


def solution(mesh):
    placed = P(("row", "depth"), "col")
    weights = P("row", "col")
    return jax.shard_map(
        body,
        mesh=mesh,
        in_specs=(placed, weights, weights, placed),
        out_specs=(placed, placed, weights, weights),
        check_vma=False,
    )
```

```python
import functools

import jax
import jax.numpy as jnp
from jax import lax
from jax.experimental import pallas as pl
from jax.experimental.pallas import tpu as pltpu
from jax.sharding import PartitionSpec as P

MESH = pl.DeviceIdType.MESH
F32 = jnp.float32
BF16 = jnp.bfloat16
C0 = 0.7978845608028654
C1 = 0.044715


def nt(left, right):
    return lax.dot_general(left, right, (((1,), (1,)), ((), ())), preferred_element_type=F32)


def nn(left, right):
    return jnp.dot(left, right, preferred_element_type=F32)


class Local:
    def __init__(self, copy):
        self.wait_recv = copy.wait


class Copies:
    def __init__(self, send, recv):
        self.send, self.recv, self.count, self.sent = send, recv, 0, []

    def make(self, src, dst, device):
        k = self.count
        self.count += 1
        return pltpu.make_async_remote_copy(
            src_ref=src,
            dst_ref=dst,
            send_sem=self.send.at[k],
            recv_sem=self.recv.at[k],
            device_id=device,
            device_id_type=MESH,
        )

    def start(self, src, dst, device):
        copy = self.make(src, dst, device)
        copy.start()
        self.sent.append(copy)
        return copy


ORDER = (
    ((0, 0), (0, 1), (0, 3), (1, 0)),
    ((3, 0), (1, 1), (1, 3), (3, 1)),
    ((3, 3), (0, 2), (2, 0), (1, 2)),
    ((3, 2), (2, 1), (2, 3), (2, 2)),
)
FLAT = [pair for group in ORDER for pair in group]
SLOT = {pair: n for n, pair in enumerate(FLAT)}


def kernel(
    tok_ref, grd_ref, win_ref, wout_ref,
    outT_ref, gtokT_ref, gwin_ref, gwout_ref,
    acts, wbuf, wt, acc, dgel, hid, gpre, terms, wpart, sib, zrecv, fin,
    rs1, ssum, rs2, send_sem, recv_sem, w_sem, bulk_send, bulk_recv, o_sem, o_send, o_recv,
):
    R, T = outT_ref.shape
    H = win_ref.shape[1]
    G = 4 * R
    half = R // 2
    row, col, z = lax.axis_index("row"), lax.axis_index("col"), lax.axis_index("depth")
    y, x = lax.div(col, 4), lax.rem(col, 4)
    other = 1 - row

    def at(yy, xx):
        return lax.rem(yy + 4, 4) * 4 + lax.rem(xx + 4, 4)

    p_plus = (row, at(y + row, x + other), z)
    p_minus = (row, at(y - row, x - other), z)
    q_plus = (row, at(y + other, x + row), z)
    q_minus = (row, at(y - other, x - row), z)
    z_plus = (row, col, lax.rem(z + 1, 8))
    z_minus = (row, col, lax.rem(z + 7, 8))
    sibling = (other, col, z)
    partners = (p_plus, p_minus, q_plus, q_minus, z_plus, z_minus, sibling)

    barrier = pltpu.get_barrier_semaphore()
    for dev in partners:
        pl.semaphore_signal(barrier, inc=1, device_id=dev, device_id_type=MESH)

    copies = Copies(send_sem, recv_sem)
    owns = [
        pltpu.make_async_copy(src, acts.at[a, pl.ds(0, R)], w_sem.at[2 + a])
        for a, src in ((0, tok_ref), (1, grd_ref))
    ]
    for cp in owns:
        cp.start()

    def offset(g, j):
        one, two = SLOT[g, j], SLOT[j, g]
        if one == two:
            return one * R
        return pl.multiple_of((one + row * (two - one)) * R, 32)

    def shard(a, g, j, lo=0, hi=None):
        hi = R if hi is None else hi
        start = offset(g, j) + lo
        if not isinstance(start, int):
            start = pl.multiple_of(start, 16)
        return acts.at[a, pl.ds(start, hi - lo)]

    got = {}

    local = [Local(cp) for cp in owns]
    got.update({(0, 0, 0): [local[0]], (1, 0, 0): [local[1]]})

    def came(a, g, j, copy):
        got.setdefault((a, g, j), []).append(copy)

    def need(a, g, j):
        for cp in got.pop((a, g, j), []):
            cp.wait_recv()

    def to_p(a):
        src = (tok_ref, grd_ref)[a]
        came(a, 0, 3, copies.start(src, shard(a, 0, 3), p_plus))
        came(a, 0, 1, copies.start(src, shard(a, 0, 1), p_minus))

    def to_q(a, j):
        if j:
            need(a, 0, j)
        src = (tok_ref, grd_ref)[a] if j == 0 else shard(a, 0, j)
        came(a, 3, j, copies.start(src, shard(a, 3, j), q_plus))
        came(a, 1, j, copies.start(src, shard(a, 1, j), q_minus))

    def pf(a, g):
        need(a, 0, g)
        lo, hi, dev = (0, half, p_plus) if g == 3 else (half, R, p_minus)
        came(a, 0, 2, copies.start(shard(a, 0, g, lo, hi), shard(a, 0, 2, lo, hi), dev))

    def qf(a, g, j):
        need(a, g, j)
        came(a, 2, j, copies.start(shard(a, g, j), shard(a, 2, j), q_plus if g == 3 else q_minus))

    def group(a, n):
        if n == 0:
            need(a, 0, 0)
        for dy, dx in ORDER[n]:
            need(a, dy, dx)
            need(a, dx, dy)

    pl.semaphore_wait(barrier, len(partners))
    def wload():
        for dy in range(4):
            place_weights(dy)

    def place_weights(dy):
        yy = lax.rem(y + dy, 4)

        @pl.when(lax.div(yy, 2) == row)
        def _():
            for dx in range(4):
                n = SLOT[dy, dx]
                start = ((yy - 2 * row) * 4 + lax.rem(x + dx, 4)) * R
                block = pl.ds(pl.multiple_of(start, 32), R)
                for w, src in ((0, win_ref), (1, wout_ref)):
                    there = wbuf.at[w, pl.ds(n * R, R)]
                    pltpu.make_async_copy(src.at[block], there, w_sem.at[w]).start()
                    pltpu.make_async_remote_copy(
                        src_ref=src.at[block], dst_ref=there, send_sem=bulk_send.at[w],
                        recv_sem=bulk_recv.at[w], device_id=sibling, device_id_type=MESH,
                    ).start()

    def trans(w):
        src = (win_ref, wout_ref)[w]
        pltpu.make_async_copy(src, wbuf.at[w, pl.ds(0, 8 * R)], w_sem.at[w]).wait()
        pltpu.make_async_remote_copy(
            src_ref=src, dst_ref=wbuf.at[w, pl.ds(0, 8 * R)], send_sem=bulk_send.at[w],
            recv_sem=bulk_recv.at[w], device_id=sibling, device_id_type=MESH,
        ).wait()

        @pl.loop(0, 4)
        def _(g):
            wt[w, g] = wbuf[w, pl.ds(pl.multiple_of(g * G, 128), G), :].T

    def project(a, n):
        group(a, n)
        part = nn(wt[a, n], acts[a, pl.ds(n * G, G), :])
        if n == 0:
            acc[...] = part
        else:
            acc[...] += part

    def rows_at(n):
        return pl.ds(n * G if isinstance(n, int) else pl.multiple_of(n * G, 128), G)

    def make_terms(a, w, src, n):
        rows = rows_at(n)
        terms[a, rows, :] = nn(wbuf[w, rows, :], src[...]).astype(BF16)

    def make_wpart(b, a, src, n):
        rows = rows_at(n)
        wpart[b, rows, :] = nt(acts[a, rows, :], src[...]).astype(BF16)

    def add(dst, srcs, rows, out=BF16):
        block = 32 if rows % 32 == 0 else 16

        @pl.loop(0, rows // block)
        def _(i):
            here = pl.multiple_of(i * block, block)
            total = None
            for ref, off in srcs:
                part = ref[pl.ds(pl.multiple_of(off + here, 16), block), :].astype(F32)
                total = part if total is None else total + part
            ref, off = dst
            ref[pl.ds(pl.multiple_of(off + here, 16), block), :] = total.astype(out)

    rs = {}

    def piece(ref, start, rows):
        if not isinstance(start, int):
            start = pl.multiple_of(start, 16)
        return ref.at[pl.ds(start, rows)]

    def rs_a(a, g, j):
        t, r = terms.at[a], rs1.at[a]
        base, dev = {1: (4, q_plus), 3: (8, q_minus)}.get(g, (0, q_plus if j < 2 else q_minus))
        key = {1: "rc", 3: "rd"}.get(g, "ra")
        rs[a, key, j] = copies.start(piece(t, offset(g, j), R), piece(r, (base + j) * R, R), dev)

    def rs_b(a, g, j):
        t, r = terms.at[a], rs1.at[a]
        rs[a, "ra", j].wait_recv()
        add((t, offset(g, j)), ((t, offset(g, j)), (r, j * R)), R)
        rs_a(a, g, j)

    def rs_c(a, j):
        t, r, s, e = terms.at[a], rs1.at[a], ssum.at[a], rs2.at[a]
        rs[a, "rc", j].wait_recv()
        rs[a, "rd", j].wait_recv()
        add((s, j * R), ((t, offset(0, j)), (r, (4 + j) * R), (r, (8 + j) * R)), R)
        if j == 2:
            rs[a, "re"] = copies.start(piece(s, 2 * R, half), piece(e, 0, half), p_plus)
            rs[a, "rf"] = copies.start(piece(s, 2 * R + half, half), piece(e, half, half), p_minus)

    def rs_d(a, j):
        s, e = ssum.at[a], rs2.at[a]
        lo, key, dev = (0, "re", p_plus) if j == 1 else (half, "rf", p_minus)
        rs[a, key].wait_recv()
        add((s, j * R + lo), ((s, j * R + lo), (e, lo)), half)
        rs[a, "last", j] = copies.start(piece(s, j * R, R), piece(e, (1 + j // 2) * R, R), dev)

    def rs_e(a):
        t, r, e, out = terms.at[a], rs1.at[a], rs2.at[a], (outT_ref, gtokT_ref)[a]
        rs[a, "rc", 0].wait_recv()
        rs[a, "rd", 0].wait_recv()
        rs[a, "last", 1].wait_recv()
        rs[a, "last", 3].wait_recv()
        add((out, 0), ((t, 0), (r, 4 * R), (r, 8 * R), (e, R), (e, 2 * R)), R)

    finals = (gwout_ref, gwin_ref)
    zs = {}

    def sign(h):
        return 1 - 2 * h

    def order(h):
        d = sign(h)
        return (4 * d, -3 * d, 3 * d, -2 * d, 2 * d, -d, d, 0)

    def chunk(delta):
        return lax.rem(z + delta + 8, 8)

    def sib_send(b, h):
        for n, delta in enumerate(order(h)):
            start = h * 8 * R + other * G + chunk(delta) * half
            zs[b, h, "sib", delta] = copies.start(
                piece(wpart.at[b], start, half), piece(sib.at[b], h * G + n * half, half), sibling
            )

    def own(b, h, delta):
        zs[b, h, "sib", delta].wait_recv()
        n = order(h).index(delta)
        mine = pl.multiple_of(h * 8 * R + row * G + chunk(delta) * half, 16)
        return ((wpart.at[b], mine), (sib.at[b], h * G + n * half))

    def ends(h, long):
        return z_plus if (sign(h) > 0) == long else z_minus

    def z_one(b, h, long, n):
        base = h * 7 + (0 if long else 4)
        delta = sign(h) * (4 - n) if long else -sign(h) * (3 - n)
        srcs = own(b, h, delta)
        if n > 0:
            zs[b, h, long, n - 1].wait_recv()
            srcs += ((zrecv.at[b], (base + n - 1) * half),)
        add(srcs[0], srcs, half)
        zs[b, h, long, n] = copies.start(
            piece(*srcs[0], half), piece(zrecv.at[b], (base + n) * half, half), ends(h, long)
        )

    def place(b, h, delta):
        return piece(fin.at[b], h * G + chunk(delta) * half, half)

    def z_final(b, h):
        srcs = own(b, h, 0)
        zs[b, h, True, 3].wait_recv()
        zs[b, h, False, 2].wait_recv()
        base = h * 7
        srcs += ((zrecv.at[b], (base + 3) * half), (zrecv.at[b], (base + 6) * half))
        add((fin.at[b], pl.multiple_of(h * G + chunk(0) * half, 16)), srcs, half)
        for long in (True, False):
            zs[b, h, "ag", long, 0] = copies.start(place(b, h, 0), place(b, h, 0), ends(h, long))

    def z_gather(b, h, long, n):
        delta = (-sign(h) if long else sign(h)) * n
        zs[b, h, "ag", long, n - 1].wait_recv()
        zs[b, h, "ag", long, n] = copies.start(place(b, h, delta), place(b, h, delta), ends(h, long))

    def owner_of(h, j, core):
        one, two = FLAT[h * 8 + j], FLAT[h * 8 + 4 + j]
        dy, dx = (p + core * (q - p) for p, q in zip(one, two))
        yy = lax.rem(y + dy, 4)
        target = lax.div(yy, 2)
        start = ((yy - 2 * target) * 4 + lax.rem(x + dx, 4)) * R
        return target, pl.ds(pl.multiple_of(start, 32), R)

    def out_here(b, h, j, rows):
        n = (b * 2 + h) * 4 + j
        return pltpu.make_async_copy(piece(fin.at[b], h * G + j * R, R), finals[b].at[rows], o_sem.at[n])

    def out_there(b, h, j, rows):
        n = (b * 2 + h) * 4 + j
        return pltpu.make_async_remote_copy(
            src_ref=piece(fin.at[b], h * G + j * R, R), dst_ref=finals[b].at[rows],
            send_sem=o_send.at[n], recv_sem=o_recv.at[n], device_id=sibling, device_id_type=MESH,
        )

    def z_end(b, h):
        zs[b, h, "ag", True, 3].wait_recv()
        zs[b, h, "ag", False, 2].wait_recv()
        for j in range(4):
            target, rows = owner_of(h, j, row)
            pl.when(target == row)(lambda: out_here(b, h, j, rows).start())
            pl.when(target != row)(lambda: out_there(b, h, j, rows).start())

    def z_stored(b, h):
        for j in range(4):
            target, rows = owner_of(h, j, row)
            pl.when(target == row)(lambda: out_here(b, h, j, rows).wait())
            pl.when(target != row)(lambda: out_there(b, h, j, rows).wait_send())
            target, rows = owner_of(h, j, other)
            pl.when(target == row)(lambda: out_there(b, h, j, rows).wait_recv())

    def gelu():
        step = 32

        @pl.loop(0, H // step)
        def _(i):
            rows = pl.ds(pl.multiple_of(i * step, step), step)
            v = acc[rows, :]
            sq = v * v
            t = jnp.tanh(C0 * (v + C1 * (sq * v)))
            cdf = 0.5 * (1.0 + t)
            hid[rows, :] = (v * cdf).astype(BF16)
            dgel[rows, :] = cdf + (0.5 * C0) * v * (1.0 - t * t) * (1.0 + (3.0 * C1) * sq)

    def gelu_back():
        step = 32

        @pl.loop(0, H // step)
        def _(i):
            rows = pl.ds(pl.multiple_of(i * step, step), step)
            gpre[rows, :] = (acc[rows, :] * dgel[rows, :]).astype(BF16)

    def wpart_o(b, h):
        if b == 0:
            group(1, 2 * h)
            group(1, 2 * h + 1)
        make_wpart(b, 1 - b, (hid, gpre)[b], 2 * h + other)

    def wpart_m(b, h):
        make_wpart(b, 1 - b, (hid, gpre)[b], 2 * h + row)

    def terms_of(a, n):
        make_terms(a, 1 - a, (hid, gpre)[a], n)

    to_p(0)
    wload()
    to_q(1, 0)
    to_p(1)
    to_q(0, 3)
    pf(0, 3)
    to_q(0, 1)
    pf(0, 1)
    to_q(0, 0)
    to_q(0, 2)
    pf(1, 1)
    qf(0, 3, 1)
    pf(1, 3)
    qf(0, 1, 3)
    to_q(1, 3)
    qf(0, 1, 2)
    qf(0, 3, 0)
    to_q(1, 1)
    trans(0)
    qf(1, 3, 0)
    trans(1)
    to_q(1, 2)
    project(0, 0)
    project(0, 1)
    project(0, 2)
    project(0, 3)
    qf(1, 1, 3)
    gelu()
    wpart_o(0, 0)
    sib_send(0, 0)
    wpart_m(0, 0)
    qf(1, 3, 1)
    terms_of(0, 0)
    z_one(0, 0, True, 0)
    qf(1, 1, 2)
    z_one(0, 0, False, 0)
    terms_of(0, 1)
    terms_of(0, 3)
    terms_of(0, 2)
    rs_a(0, 2, 0)
    rs_a(0, 3, 0)
    project(1, 0)
    project(1, 1)
    z_one(0, 0, True, 1)
    rs_a(0, 2, 2)
    z_one(0, 0, False, 1)
    wpart_o(0, 1)
    sib_send(0, 1)
    wpart_m(0, 1)
    project(1, 2)
    z_one(0, 1, True, 0)
    z_one(0, 1, False, 0)
    project(1, 3)
    gelu_back()
    wpart_o(1, 0)
    z_one(0, 0, True, 2)
    z_one(0, 0, False, 2)
    sib_send(1, 0)
    wpart_m(1, 0)
    terms_of(1, 3)
    z_one(1, 0, False, 0)
    z_one(1, 0, True, 0)
    z_one(0, 1, False, 1)
    z_one(0, 1, True, 1)
    wpart_o(1, 1)
    terms_of(1, 2)
    sib_send(1, 1)
    rs_a(0, 1, 2)
    terms_of(1, 0)
    rs_a(0, 2, 1)
    wpart_m(1, 1)
    z_one(1, 1, False, 0)
    terms_of(1, 1)
    rs_a(1, 1, 3)
    rs_a(1, 2, 0)
    z_one(1, 1, True, 0)
    rs_a(1, 2, 3)
    rs_a(0, 2, 3)
    rs_b(0, 3, 2)
    z_one(0, 0, True, 3)
    z_one(1, 0, True, 1)
    rs_a(1, 2, 2)
    z_one(0, 1, True, 2)
    z_one(1, 1, True, 1)
    z_one(1, 1, False, 1)
    z_one(1, 0, False, 1)
    rs_a(1, 2, 1)
    rs_a(0, 1, 3)
    rs_b(0, 1, 0)
    z_one(0, 1, False, 2)
    rs_a(1, 3, 1)
    z_one(1, 1, True, 2)
    rs_a(0, 3, 1)
    z_one(0, 1, True, 3)
    z_one(1, 0, False, 2)
    z_one(1, 0, True, 2)
    rs_b(1, 3, 3)
    z_final(0, 0)
    z_one(1, 0, True, 3)
    rs_b(1, 1, 1)
    z_one(1, 1, True, 3)
    rs_c(0, 2)
    z_one(1, 1, False, 2)
    rs_a(1, 1, 2)
    z_final(0, 1)
    z_gather(0, 0, True, 1)
    z_final(1, 0)
    rs_b(0, 1, 1)
    rs_b(0, 3, 3)
    z_gather(0, 1, True, 1)
    rs_b(1, 3, 2)
    z_gather(0, 1, False, 1)
    z_final(1, 1)
    z_gather(0, 0, False, 1)
    rs_c(0, 3)
    z_gather(1, 0, True, 1)
    z_gather(0, 0, True, 2)
    z_gather(0, 1, True, 2)
    z_gather(0, 1, False, 2)
    rs_c(0, 1)
    rs_b(1, 1, 0)
    rs_a(1, 3, 0)
    rs_d(0, 3)
    z_gather(1, 1, True, 1)
    rs_c(1, 2)
    z_gather(1, 0, False, 1)
    z_gather(0, 1, True, 3)
    z_gather(1, 0, True, 2)
    rs_c(1, 3)
    z_gather(1, 1, True, 2)
    z_gather(1, 1, False, 1)
    z_gather(0, 0, False, 2)
    z_gather(0, 0, True, 3)
    rs_c(1, 1)
    rs_d(0, 1)
    z_gather(1, 0, True, 3)
    rs_e(0)
    rs_d(1, 3)
    z_gather(1, 0, False, 2)
    z_gather(1, 1, True, 3)
    z_gather(1, 1, False, 2)
    z_end(0, 1)
    z_end(0, 0)
    rs_d(1, 1)
    z_stored(0, 1)
    z_end(1, 0)
    z_stored(0, 0)
    z_end(1, 1)
    rs_e(1)
    z_stored(1, 0)
    z_stored(1, 1)
    for cp in copies.sent:
        cp.wait_send()


def settle(*refs):
    sems = refs[8]
    moves = []
    for src, dst in zip(refs[:4], refs[4:8]):
        parts = 1 if src.shape[0] < 512 else 4
        rows = src.shape[0] // parts
        for i in range(parts):
            here = pl.ds(i * rows, rows)
            moves.append(pltpu.make_async_copy(src.at[here], dst.at[here], sems.at[len(moves)]))
    for move in moves:
        move.start()
    for move in moves:
        move.wait()


N_COPIES = 2 * 16 + 2 * 16 + 4 * (8 + 7 + 7)


def body(tokens_in, w_in, w_out, grad_out):
    T, R = tokens_in.shape
    H = w_in.shape[1]
    tokT, grdT = tokens_in.T, grad_out.T
    vmem = pl.BlockSpec(memory_space=pltpu.VMEM)
    hbm = pl.BlockSpec(memory_space=pl.ANY)
    outT, gtokT, g_in, g_out = pl.pallas_call(
        kernel,
        out_shape=(
            pltpu.VMEM((R, T), BF16),
            pltpu.VMEM((R, T), BF16),
            pltpu.VMEM(w_in.shape, BF16),
            pltpu.VMEM(w_out.shape, BF16),
        ),
        in_specs=[hbm] * 4,
        out_specs=(vmem,) * 4,
        scratch_shapes=[
            pltpu.VMEM((2, 16 * R, T), BF16),
            pltpu.VMEM((2, 16 * R, H), BF16),
            pltpu.VMEM((2, 4, H, 4 * R), BF16),
            pltpu.VMEM((H, T), F32),
            pltpu.VMEM((H, T), F32),
            pltpu.VMEM((H, T), BF16),
            pltpu.VMEM((H, T), BF16),
            pltpu.VMEM((2, 16 * R, T), BF16),
            pltpu.VMEM((2, 16 * R, H), BF16),
            pltpu.VMEM((2, 8 * R, H), BF16),
            pltpu.VMEM((2, 7 * R, H), BF16),
            pltpu.VMEM((2, 8 * R, H), BF16),
            pltpu.VMEM((2, 12 * R, T), BF16),
            pltpu.VMEM((2, 4 * R, T), BF16),
            pltpu.VMEM((2, 3 * R, T), BF16),
            pltpu.SemaphoreType.DMA((N_COPIES,)),
            pltpu.SemaphoreType.DMA((N_COPIES,)),
            pltpu.SemaphoreType.DMA((4,)),
            pltpu.SemaphoreType.DMA((2,)),
            pltpu.SemaphoreType.DMA((2,)),
            pltpu.SemaphoreType.DMA((16,)),
            pltpu.SemaphoreType.DMA((16,)),
            pltpu.SemaphoreType.DMA((16,)),
        ],
        compiler_params=pltpu.CompilerParams(
            collective_id=0, has_side_effects=True, vmem_limit_bytes=54 * 1024 * 1024
        ),
    )(tokT, grdT, w_in, w_out)
    arrays = tuple(pltpu.with_memory_space_constraint(a, pltpu.VMEM) for a in (outT, gtokT, g_in, g_out))
    outT, gtokT, g_in, g_out = pl.pallas_call(
        settle,
        out_shape=tuple(jax.ShapeDtypeStruct(a.shape, BF16) for a in arrays),
        in_specs=[vmem] * 4,
        out_specs=(hbm,) * 4,
        scratch_shapes=[pltpu.SemaphoreType.DMA((10,))],
        compiler_params=pltpu.CompilerParams(vmem_limit_bytes=4 * 1024 * 1024),
    )(*arrays)
    return outT.T, gtokT.T, g_in, g_out


def solution(mesh):
    placed = P(("row", "depth"), "col")
    weights = P("row", "col")
    return jax.shard_map(
        body,
        mesh=mesh,
        in_specs=(placed, weights, weights, placed),
        out_specs=(placed, placed, weights, weights),
        check_vma=False,
    )
```

```python
import functools

import jax
import jax.numpy as jnp
from jax import lax
from jax.experimental import pallas as pl
from jax.experimental.pallas import tpu as pltpu
from jax.sharding import PartitionSpec as P

MESH = pl.DeviceIdType.MESH
F32 = jnp.float32
BF16 = jnp.bfloat16
C0 = 0.7978845608028654
C1 = 0.044715


def nt(left, right):
    return lax.dot_general(left, right, (((1,), (1,)), ((), ())), preferred_element_type=F32)


def nn(left, right):
    return jnp.dot(left, right, preferred_element_type=F32)


class Local:
    def __init__(self, copy):
        self.wait_recv = copy.wait


class Copies:
    def __init__(self, send, recv):
        self.send, self.recv, self.count, self.sent = send, recv, 0, []

    def make(self, src, dst, device):
        k = self.count
        self.count += 1
        return pltpu.make_async_remote_copy(
            src_ref=src,
            dst_ref=dst,
            send_sem=self.send.at[k],
            recv_sem=self.recv.at[k],
            device_id=device,
            device_id_type=MESH,
        )

    def start(self, src, dst, device):
        copy = self.make(src, dst, device)
        copy.start()
        self.sent.append(copy)
        return copy

    def flush(self, keep):
        while len(self.sent) > keep:
            self.sent.pop(0).wait_send()


ORDER = (
    ((0, 0), (0, 1), (0, 3), (1, 0)),
    ((3, 0), (1, 1), (1, 3), (3, 1)),
    ((3, 3), (0, 2), (2, 0), (1, 2)),
    ((3, 2), (2, 1), (2, 3), (2, 2)),
)
FLAT = [pair for group in ORDER for pair in group]
SLOT = {pair: n for n, pair in enumerate(FLAT)}


def kernel(
    tok_ref, grd_ref, win_ref, wout_ref,
    outT_ref, gtokT_ref, gwin_ref, gwout_ref,
    acts, wbuf, wt, acc, dgel, hid, gpre, terms, wpart, sib, zrecv, fin,
    rs1, ssum, rs2, send_sem, recv_sem, w_sem, bulk_send, bulk_recv, o_sem, o_send, o_recv,
):
    R, T = outT_ref.shape
    H = win_ref.shape[1]
    G = 4 * R
    half = R // 2
    row, col, z = lax.axis_index("row"), lax.axis_index("col"), lax.axis_index("depth")
    y, x = lax.div(col, 4), lax.rem(col, 4)
    other = 1 - row

    def at(yy, xx):
        return lax.rem(yy + 4, 4) * 4 + lax.rem(xx + 4, 4)

    p_plus = (row, at(y + row, x + other), z)
    p_minus = (row, at(y - row, x - other), z)
    q_plus = (row, at(y + other, x + row), z)
    q_minus = (row, at(y - other, x - row), z)
    z_plus = (row, col, lax.rem(z + 1, 8))
    z_minus = (row, col, lax.rem(z + 7, 8))
    sibling = (other, col, z)
    partners = (p_plus, p_minus, q_plus, q_minus, z_plus, z_minus, sibling)

    barrier = pltpu.get_barrier_semaphore()
    for dev in partners:
        pl.semaphore_signal(barrier, inc=1, device_id=dev, device_id_type=MESH)

    copies = Copies(send_sem, recv_sem)
    owns = [
        pltpu.make_async_copy(src, acts.at[a, pl.ds(0, R)], w_sem.at[2 + a])
        for a, src in ((0, tok_ref), (1, grd_ref))
    ]
    for cp in owns:
        cp.start()

    def offset(g, j):
        one, two = SLOT[g, j], SLOT[j, g]
        if one == two:
            return one * R
        return pl.multiple_of((one + row * (two - one)) * R, 32)

    def shard(a, g, j, lo=0, hi=None):
        hi = R if hi is None else hi
        start = offset(g, j) + lo
        if not isinstance(start, int):
            start = pl.multiple_of(start, 16)
        return acts.at[a, pl.ds(start, hi - lo)]

    got = {}

    local = [Local(cp) for cp in owns]
    got.update({(0, 0, 0): [local[0]], (1, 0, 0): [local[1]]})

    def came(a, g, j, copy):
        got.setdefault((a, g, j), []).append(copy)

    def need(a, g, j):
        for cp in got.pop((a, g, j), []):
            cp.wait_recv()

    def to_p(a):
        need(a, 0, 0)
        src = shard(a, 0, 0)
        came(a, 0, 3, copies.start(src, shard(a, 0, 3), p_plus))
        came(a, 0, 1, copies.start(src, shard(a, 0, 1), p_minus))

    def to_q(a, j):
        need(a, 0, j)
        src = shard(a, 0, j)
        came(a, 3, j, copies.start(src, shard(a, 3, j), q_plus))
        came(a, 1, j, copies.start(src, shard(a, 1, j), q_minus))

    def pf(a, g):
        need(a, 0, g)
        lo, hi, dev = (0, half, p_plus) if g == 3 else (half, R, p_minus)
        came(a, 0, 2, copies.start(shard(a, 0, g, lo, hi), shard(a, 0, 2, lo, hi), dev))

    def qf(a, g, j):
        need(a, g, j)
        came(a, 2, j, copies.start(shard(a, g, j), shard(a, 2, j), q_plus if g == 3 else q_minus))

    def group(a, n):
        if n == 0:
            need(a, 0, 0)
        for dy, dx in ORDER[n]:
            need(a, dy, dx)
            need(a, dx, dy)

    pl.semaphore_wait(barrier, len(partners))
    def wload():
        for dy in range(4):
            place_weights(dy)

    def place_weights(dy):
        yy = lax.rem(y + dy, 4)

        @pl.when(lax.div(yy, 2) == row)
        def _():
            for dx in range(4):
                n = SLOT[dy, dx]
                start = ((yy - 2 * row) * 4 + lax.rem(x + dx, 4)) * R
                block = pl.ds(pl.multiple_of(start, 32), R)
                for w, src in ((0, win_ref), (1, wout_ref)):
                    there = wbuf.at[w, pl.ds(n * R, R)]
                    pltpu.make_async_copy(src.at[block], there, w_sem.at[w]).start()
                    pltpu.make_async_remote_copy(
                        src_ref=src.at[block], dst_ref=there, send_sem=bulk_send.at[w],
                        recv_sem=bulk_recv.at[w], device_id=sibling, device_id_type=MESH,
                    ).start()

    def trans(w):
        src = (win_ref, wout_ref)[w]
        pltpu.make_async_copy(src, wbuf.at[w, pl.ds(0, 8 * R)], w_sem.at[w]).wait()
        pltpu.make_async_remote_copy(
            src_ref=src, dst_ref=wbuf.at[w, pl.ds(0, 8 * R)], send_sem=bulk_send.at[w],
            recv_sem=bulk_recv.at[w], device_id=sibling, device_id_type=MESH,
        ).wait()

        @pl.loop(0, 4)
        def _(g):
            wt[w, g] = wbuf[w, pl.ds(pl.multiple_of(g * G, 128), G), :].T

    def project(a, n):
        group(a, n)
        part = nn(wt[a, n], acts[a, pl.ds(n * G, G), :])
        if n == 0:
            acc[...] = part
        else:
            acc[...] += part

    def rows_at(n):
        return pl.ds(n * G if isinstance(n, int) else pl.multiple_of(n * G, 128), G)

    def make_terms(a, w, src, n):
        rows = rows_at(n)
        terms[a, rows, :] = nn(wbuf[w, rows, :], src[...]).astype(BF16)

    def make_wpart(b, a, src, n):
        rows = rows_at(n)
        wpart[b, rows, :] = nt(acts[a, rows, :], src[...]).astype(BF16)

    def add(dst, srcs, rows, out=BF16):
        block = 32 if rows % 32 == 0 else 16

        @pl.loop(0, rows // block)
        def _(i):
            here = pl.multiple_of(i * block, block)
            total = None
            for ref, off in srcs:
                part = ref[pl.ds(pl.multiple_of(off + here, 16), block), :].astype(F32)
                total = part if total is None else total + part
            ref, off = dst
            ref[pl.ds(pl.multiple_of(off + here, 16), block), :] = total.astype(out)

    rs = {}

    def piece(ref, start, rows):
        if not isinstance(start, int):
            start = pl.multiple_of(start, 16)
        return ref.at[pl.ds(start, rows)]

    def rs_a(a, g, j):
        t, r = terms.at[a], rs1.at[a]
        base, dev = {1: (4, q_plus), 3: (8, q_minus)}.get(g, (0, q_plus if j < 2 else q_minus))
        key = {1: "rc", 3: "rd"}.get(g, "ra")
        rs[a, key, j] = copies.start(piece(t, offset(g, j), R), piece(r, (base + j) * R, R), dev)

    def rs_b(a, g, j):
        t, r = terms.at[a], rs1.at[a]
        rs[a, "ra", j].wait_recv()
        add((t, offset(g, j)), ((t, offset(g, j)), (r, j * R)), R)
        rs_a(a, g, j)

    def rs_c(a, j):
        t, r, s, e = terms.at[a], rs1.at[a], ssum.at[a], rs2.at[a]
        rs[a, "rc", j].wait_recv()
        rs[a, "rd", j].wait_recv()
        add((s, j * R), ((t, offset(0, j)), (r, (4 + j) * R), (r, (8 + j) * R)), R)
        if j == 2:
            rs[a, "re"] = copies.start(piece(s, 2 * R, half), piece(e, 0, half), p_plus)
            rs[a, "rf"] = copies.start(piece(s, 2 * R + half, half), piece(e, half, half), p_minus)

    def rs_d(a, j):
        s, e = ssum.at[a], rs2.at[a]
        lo, key, dev = (0, "re", p_plus) if j == 1 else (half, "rf", p_minus)
        rs[a, key].wait_recv()
        add((s, j * R + lo), ((s, j * R + lo), (e, lo)), half)
        rs[a, "last", j] = copies.start(piece(s, j * R, R), piece(e, (1 + j // 2) * R, R), dev)

    def rs_e(a):
        t, r, e, out = terms.at[a], rs1.at[a], rs2.at[a], (outT_ref, gtokT_ref)[a]
        rs[a, "rc", 0].wait_recv()
        rs[a, "rd", 0].wait_recv()
        rs[a, "last", 1].wait_recv()
        rs[a, "last", 3].wait_recv()
        add((out, 0), ((t, 0), (r, 4 * R), (r, 8 * R), (e, R), (e, 2 * R)), R)

    finals = (gwout_ref, gwin_ref)
    zs = {}

    def sign(h):
        return 1 - 2 * h

    def order(h):
        d = sign(h)
        return (4 * d, -3 * d, 3 * d, -2 * d, 2 * d, -d, d, 0)

    def chunk(delta):
        return lax.rem(z + delta + 8, 8)

    def sib_send(b, h):
        for n, delta in enumerate(order(h)):
            start = h * 8 * R + other * G + chunk(delta) * half
            zs[b, h, "sib", delta] = copies.start(
                piece(wpart.at[b], start, half), piece(sib.at[b], h * G + n * half, half), sibling
            )

    def own(b, h, delta):
        zs[b, h, "sib", delta].wait_recv()
        n = order(h).index(delta)
        mine = pl.multiple_of(h * 8 * R + row * G + chunk(delta) * half, 16)
        return ((wpart.at[b], mine), (sib.at[b], h * G + n * half))

    def ends(h, long):
        return z_plus if (sign(h) > 0) == long else z_minus

    def z_one(b, h, long, n):
        base = h * 7 + (0 if long else 4)
        delta = sign(h) * (4 - n) if long else -sign(h) * (3 - n)
        srcs = own(b, h, delta)
        if n > 0:
            zs[b, h, long, n - 1].wait_recv()
            srcs += ((zrecv.at[b], (base + n - 1) * half),)
        add(srcs[0], srcs, half)
        zs[b, h, long, n] = copies.start(
            piece(*srcs[0], half), piece(zrecv.at[b], (base + n) * half, half), ends(h, long)
        )

    def place(b, h, delta):
        return piece(fin.at[b], h * G + chunk(delta) * half, half)

    def z_final(b, h):
        srcs = own(b, h, 0)
        zs[b, h, True, 3].wait_recv()
        zs[b, h, False, 2].wait_recv()
        base = h * 7
        srcs += ((zrecv.at[b], (base + 3) * half), (zrecv.at[b], (base + 6) * half))
        add((fin.at[b], pl.multiple_of(h * G + chunk(0) * half, 16)), srcs, half)
        for long in (True, False):
            zs[b, h, "ag", long, 0] = copies.start(place(b, h, 0), place(b, h, 0), ends(h, long))

    def z_gather(b, h, long, n):
        delta = (-sign(h) if long else sign(h)) * n
        zs[b, h, "ag", long, n - 1].wait_recv()
        zs[b, h, "ag", long, n] = copies.start(place(b, h, delta), place(b, h, delta), ends(h, long))

    def owner_of(h, j, core):
        one, two = FLAT[h * 8 + j], FLAT[h * 8 + 4 + j]
        dy, dx = (p + core * (q - p) for p, q in zip(one, two))
        yy = lax.rem(y + dy, 4)
        target = lax.div(yy, 2)
        start = ((yy - 2 * target) * 4 + lax.rem(x + dx, 4)) * R
        return target, pl.ds(pl.multiple_of(start, 32), R)

    def out_here(b, h, j, rows):
        n = (b * 2 + h) * 4 + j
        return pltpu.make_async_copy(piece(fin.at[b], h * G + j * R, R), finals[b].at[rows], o_sem.at[n])

    def out_there(b, h, j, rows):
        n = (b * 2 + h) * 4 + j
        return pltpu.make_async_remote_copy(
            src_ref=piece(fin.at[b], h * G + j * R, R), dst_ref=finals[b].at[rows],
            send_sem=o_send.at[n], recv_sem=o_recv.at[n], device_id=sibling, device_id_type=MESH,
        )

    def z_end(b, h):
        zs[b, h, "ag", True, 3].wait_recv()
        zs[b, h, "ag", False, 2].wait_recv()
        for j in range(4):
            target, rows = owner_of(h, j, row)
            pl.when(target == row)(lambda: out_here(b, h, j, rows).start())
            pl.when(target != row)(lambda: out_there(b, h, j, rows).start())

    def z_stored(b, h):
        for j in range(4):
            target, rows = owner_of(h, j, row)
            pl.when(target == row)(lambda: out_here(b, h, j, rows).wait())
            pl.when(target != row)(lambda: out_there(b, h, j, rows).wait_send())
            target, rows = owner_of(h, j, other)
            pl.when(target == row)(lambda: out_there(b, h, j, rows).wait_recv())

    def gelu():
        step = 32

        @pl.loop(0, H // step)
        def _(i):
            rows = pl.ds(pl.multiple_of(i * step, step), step)
            v = acc[rows, :]
            sq = v * v
            t = jnp.tanh(C0 * (v + C1 * (sq * v)))
            cdf = 0.5 * (1.0 + t)
            hid[rows, :] = (v * cdf).astype(BF16)
            dgel[rows, :] = cdf + (0.5 * C0) * v * (1.0 - t * t) * (1.0 + (3.0 * C1) * sq)

    def gelu_back():
        step = 32

        @pl.loop(0, H // step)
        def _(i):
            rows = pl.ds(pl.multiple_of(i * step, step), step)
            gpre[rows, :] = (acc[rows, :] * dgel[rows, :]).astype(BF16)

    def wpart_o(b, h):
        if b == 0:
            group(1, 2 * h)
            group(1, 2 * h + 1)
        make_wpart(b, 1 - b, (hid, gpre)[b], 2 * h + other)

    def wpart_m(b, h):
        make_wpart(b, 1 - b, (hid, gpre)[b], 2 * h + row)

    def terms_of(a, n):
        make_terms(a, 1 - a, (hid, gpre)[a], n)

    to_p(0)
    to_q(0, 0)
    to_q(1, 0)
    to_p(1)
    qf(0, 3, 0)
    to_q(0, 1)
    pf(0, 1)
    pf(0, 3)
    to_q(0, 3)
    wload()
    pf(1, 3)
    pf(1, 1)
    to_q(0, 2)
    to_q(1, 1)
    qf(0, 1, 3)
    trans(0)
    qf(0, 3, 1)
    qf(0, 1, 2)
    to_q(1, 3)
    project(0, 0)
    trans(1)
    qf(1, 3, 1)
    to_q(1, 2)
    project(0, 1)
    project(0, 2)
    project(0, 3)
    gelu()
    qf(1, 1, 3)
    wpart_o(0, 0)
    sib_send(0, 0)
    wpart_m(0, 0)
    qf(1, 3, 0)
    qf(1, 1, 2)
    terms_of(0, 2)
    z_one(0, 0, True, 0)
    z_one(0, 0, False, 0)
    terms_of(0, 1)
    project(1, 0)
    project(1, 1)
    terms_of(0, 3)
    terms_of(0, 0)
    wpart_o(0, 1)
    z_one(0, 0, True, 1)
    z_one(0, 0, False, 1)
    sib_send(0, 1)
    project(1, 2)
    project(1, 3)
    wpart_m(0, 1)
    z_one(0, 1, True, 0)
    z_one(0, 1, False, 0)
    gelu_back()
    wpart_o(1, 1)
    sib_send(1, 1)
    rs_a(0, 2, 0)
    z_one(0, 0, True, 2)
    wpart_m(1, 1)
    z_one(1, 1, True, 0)
    z_one(0, 1, True, 1)
    z_one(1, 1, False, 0)
    wpart_o(1, 0)
    sib_send(1, 0)
    wpart_m(1, 0)
    rs_a(0, 2, 1)
    z_one(0, 0, False, 2)
    z_one(0, 1, False, 1)
    rs_a(0, 2, 2)
    terms_of(1, 3)
    z_one(0, 0, True, 3)
    z_one(1, 0, True, 0)
    terms_of(1, 1)
    z_one(0, 1, True, 2)
    rs_a(0, 3, 0)
    terms_of(1, 2)
    terms_of(1, 0)
    rs_a(1, 1, 3)
    rs_a(1, 2, 3)
    z_one(1, 0, False, 0)
    z_one(0, 1, False, 2)
    z_final(0, 0)
    rs_a(1, 2, 2)
    rs_a(1, 1, 2)
    z_one(1, 1, False, 1)
    rs_a(0, 3, 1)
    rs_a(0, 2, 3)
    rs_b(0, 1, 0)
    rs_b(0, 1, 1)
    rs_a(0, 1, 2)
    z_one(0, 1, True, 3)
    z_one(1, 1, True, 1)
    z_gather(0, 0, False, 1)
    z_one(1, 0, True, 1)
    rs_b(1, 3, 3)
    z_one(1, 0, False, 1)
    rs_a(1, 2, 0)
    z_final(0, 1)
    rs_a(1, 3, 1)
    rs_a(0, 1, 3)
    rs_b(1, 3, 2)
    z_one(1, 1, False, 2)
    z_one(1, 1, True, 2)
    rs_a(1, 2, 1)
    z_one(1, 0, True, 2)
    z_gather(0, 0, True, 1)
    rs_b(0, 3, 2)
    z_gather(0, 0, False, 2)
    rs_b(0, 3, 3)
    rs_c(1, 3)
    rs_b(1, 1, 0)
    z_one(1, 0, False, 2)
    rs_c(0, 1)
    z_one(1, 0, True, 3)
    z_one(1, 1, True, 3)
    z_gather(0, 0, True, 2)
    rs_b(1, 1, 1)
    rs_c(0, 2)
    z_final(1, 0)
    z_final(1, 1)
    rs_c(1, 2)
    z_gather(0, 1, True, 1)
    rs_d(0, 1)
    z_gather(0, 0, True, 3)
    rs_c(0, 3)
    rs_c(1, 1)
    rs_d(0, 3)
    z_gather(0, 1, False, 1)
    z_gather(1, 0, True, 1)
    rs_a(1, 3, 0)
    rs_d(1, 3)
    z_gather(1, 1, True, 1)
    z_gather(0, 1, True, 2)
    rs_d(1, 1)
    copies.flush(40)
    z_end(0, 0)
    z_gather(1, 1, False, 1)
    z_gather(1, 0, False, 1)
    z_gather(1, 1, True, 2)
    z_gather(1, 0, True, 2)
    rs_e(0)
    z_stored(0, 0)
    rs_e(1)
    z_gather(0, 1, True, 3)
    z_gather(0, 1, False, 2)
    z_gather(1, 0, False, 2)
    z_gather(1, 0, True, 3)
    z_gather(1, 1, True, 3)
    z_gather(1, 1, False, 2)
    z_end(0, 1)
    z_end(1, 0)
    z_stored(0, 1)
    copies.flush(8)
    z_end(1, 1)
    z_stored(1, 0)
    z_stored(1, 1)
    copies.flush(0)


def settle(*refs):
    sems = refs[8]
    moves = []
    for src, dst in zip(refs[:4], refs[4:8]):
        parts = 1 if src.shape[0] < 512 else 4
        rows = src.shape[0] // parts
        for i in range(parts):
            here = pl.ds(i * rows, rows)
            moves.append(pltpu.make_async_copy(src.at[here], dst.at[here], sems.at[len(moves)]))
    for move in moves:
        move.start()
    for move in moves:
        move.wait()


N_COPIES = 2 * 16 + 2 * 16 + 4 * (8 + 7 + 7)


def body(tokens_in, w_in, w_out, grad_out):
    T, R = tokens_in.shape
    H = w_in.shape[1]
    tokT, grdT = tokens_in.T, grad_out.T
    vmem = pl.BlockSpec(memory_space=pltpu.VMEM)
    hbm = pl.BlockSpec(memory_space=pl.ANY)
    outT, gtokT, g_in, g_out = pl.pallas_call(
        kernel,
        out_shape=(
            pltpu.VMEM((R, T), BF16),
            pltpu.VMEM((R, T), BF16),
            pltpu.VMEM(w_in.shape, BF16),
            pltpu.VMEM(w_out.shape, BF16),
        ),
        in_specs=[hbm] * 4,
        out_specs=(vmem,) * 4,
        scratch_shapes=[
            pltpu.VMEM((2, 16 * R, T), BF16),
            pltpu.VMEM((2, 16 * R, H), BF16),
            pltpu.VMEM((2, 4, H, 4 * R), BF16),
            pltpu.VMEM((H, T), F32),
            pltpu.VMEM((H, T), F32),
            pltpu.VMEM((H, T), BF16),
            pltpu.VMEM((H, T), BF16),
            pltpu.VMEM((2, 16 * R, T), BF16),
            pltpu.VMEM((2, 16 * R, H), BF16),
            pltpu.VMEM((2, 8 * R, H), BF16),
            pltpu.VMEM((2, 7 * R, H), BF16),
            pltpu.VMEM((2, 8 * R, H), BF16),
            pltpu.VMEM((2, 12 * R, T), BF16),
            pltpu.VMEM((2, 4 * R, T), BF16),
            pltpu.VMEM((2, 3 * R, T), BF16),
            pltpu.SemaphoreType.DMA((N_COPIES,)),
            pltpu.SemaphoreType.DMA((N_COPIES,)),
            pltpu.SemaphoreType.DMA((4,)),
            pltpu.SemaphoreType.DMA((2,)),
            pltpu.SemaphoreType.DMA((2,)),
            pltpu.SemaphoreType.DMA((16,)),
            pltpu.SemaphoreType.DMA((16,)),
            pltpu.SemaphoreType.DMA((16,)),
        ],
        compiler_params=pltpu.CompilerParams(
            collective_id=0, has_side_effects=True, vmem_limit_bytes=54 * 1024 * 1024
        ),
    )(tokT, grdT, w_in, w_out)
    arrays = tuple(pltpu.with_memory_space_constraint(a, pltpu.VMEM) for a in (outT, gtokT, g_in, g_out))
    outT, gtokT, g_in, g_out = pl.pallas_call(
        settle,
        out_shape=tuple(jax.ShapeDtypeStruct(a.shape, BF16) for a in arrays),
        in_specs=[vmem] * 4,
        out_specs=(hbm,) * 4,
        scratch_shapes=[pltpu.SemaphoreType.DMA((10,))],
        compiler_params=pltpu.CompilerParams(vmem_limit_bytes=4 * 1024 * 1024),
    )(*arrays)
    return outT.T, gtokT.T, g_in, g_out


def solution(mesh):
    placed = P(("row", "depth"), "col")
    weights = P("row", "col")
    return jax.shard_map(
        body,
        mesh=mesh,
        in_specs=(placed, weights, weights, placed),
        out_specs=(placed, placed, weights, weights),
        check_vma=False,
    )
```
